256 devices in a mesh: dp: 16 (over y, z_lo), tensor: 16 (over z_hi, x, core).
Axes of the slice: x: 4, y: 4, z: 8 (z_hi: 2, z_lo: 4; z = z_hi * 4 + z_lo), core: 2. Of those that a mesh axis runs over, the one named last changes fastest.
Arguments:
- inputs: bfloat16 [4096, 2560], P(('dp', 'tensor')), may hold values from -6 to 6
- gate_weight: bfloat16 [2560, 12800], P(None, 'tensor'), may hold values from -0.125 to 0.125
- up_weight: bfloat16 [2560, 12800], P(None, 'tensor'), may hold values from -0.125 to 0.125
- down_weight: bfloat16 [12800, 2560], P('tensor'), may hold values from -0.0546875 to 0.0546875
- gate_adapter_in: bfloat16 [2560, 32], replicated, may hold values from -0.125 to 0.125
- b_gate: bfloat16 [32, 12800], P(None, 'tensor'), may hold values from -0.29882812 to 0.29882812
- upper_adapter_in: bfloat16 [2560, 32], replicated, may hold values from -0.125 to 0.125
- b_up: bfloat16 [32, 12800], P(None, 'tensor'), may hold values from -0.29882812 to 0.29882812
- down_adapter_in: bfloat16 [12800, 32], P('tensor'), may hold values from -0.0546875 to 0.0546875
- b_down: bfloat16 [32, 2560], replicated, may hold values from -0.29882812 to 0.29882812
- m_gate: float32 [12800], P('tensor'), may hold values from 0.5 to 2
- m_up: float32 [12800], P('tensor'), may hold values from 0.5 to 2
- m_down: float32 [2560], replicated, may hold values from 0.5 to 2
- cotangent: bfloat16 [4096, 2560], P(('dp', 'tensor')), may hold values from -6 to 6
Outputs:
- outputs: bfloat16 [4096, 2560], P(('dp', 'tensor'))
- input_gradient: bfloat16 [4096, 2560], P(('dp', 'tensor'))
- gate_adapter_in_gradient: float32 [2560, 32], P(('dp', 'tensor'))
- upper_adapter_in_gradient: float32 [2560, 32], P(('dp', 'tensor'))
- gate_adapter_out_gradient: float32 [32, 12800], P(None, 'tensor')
- upper_adapter_out_gradient: float32 [32, 12800], P(None, 'tensor')
- down_adapter_in_gradient: float32 [12800, 32], P('tensor')
- down_adapter_out_gradient: float32 [32, 2560], P(None, ('dp', 'tensor'))
- grad_m_gate: float32 [12800], P('tensor')
- grad_m_up: float32 [12800], P('tensor')
- grad_m_down: float32 [2560], P(('dp', 'tensor'))
The draws below stay inside these ranges and needn't reach their ends.
All inputs are finite; a program needn't handle non-finite values.
Results may differ from the reference program's by a relative error of at most 0.024.
Values may be sent and summed in bfloat16 or wider, within the bound.
No kernel may reach another device: no remote copies, remote signals or barrier semaphores. Data moves between devices by JAX's collectives and lax.ppermute only.
A program may use at most 128 MiB of HBM per device.

```python
import math
import jax
import jax.numpy as jnp
from jax import lax

D = 2560
FF = 12800
R = 32
TOKENS = 4096


def block_scale(stream_key, extent, split, smallest, largest):
    level = 1.0
    for dim, parts in split:
        steps = jax.random.uniform(jax.random.fold_in(jax.random.fold_in(stream_key, 6), dim), (parts,), jnp.float32, smallest / len(split), largest / len(split))
        level = level * jnp.repeat(jnp.exp(steps), extent[dim] // parts).reshape((-1,) + (1,) * (len(extent) - 1 - dim))
    return level


def bell_draw(key, dims, deviation, most, cuts=(), held_as=jnp.bfloat16):
    result = jax.random.normal(key, dims, jnp.float32) * deviation
    if len(cuts) > 0:
        result = block_scale(key, dims, cuts, -0.22, 0.18) * result
    return jnp.clip(result, min=-most, max=most).astype(held_as)


def setup_inputs(seed: int = 0) -> dict:
    keys = jax.random.split(jax.random.key(seed), 15)
    return {
        "inputs": bell_draw(keys[0], (TOKENS, D), 1.0, 6.0, ((0, 256),)),
        "gate_weight": bell_draw(keys[1], (D, FF), D ** -0.5, 0.125, ((1, 16),)),
        "up_weight": bell_draw(keys[2], (D, FF), D ** -0.5, 0.125, ((1, 16),)),
        "down_weight": bell_draw(keys[3], (FF, D), FF ** -0.5, 0.0546875, ((0, 16),)),
        "gate_adapter_in": bell_draw(keys[4], (D, R), D ** -0.5, 0.125),
        "b_gate": bell_draw(keys[5], (R, FF), 0.05, 0.29882812, ((1, 16),)),
        "upper_adapter_in": bell_draw(keys[6], (D, R), D ** -0.5, 0.125),
        "b_up": bell_draw(keys[7], (R, FF), 0.05, 0.29882812, ((1, 16),)),
        "down_adapter_in": bell_draw(keys[8], (FF, R), FF ** -0.5, 0.0546875, ((0, 16),)),
        "b_down": bell_draw(keys[9], (R, D), 0.05, 0.29882812),
        "m_gate": jnp.clip(jnp.exp(math.log(2.0) - 1.3862944 * jax.random.uniform(keys[10], (FF,), jnp.float32) ** block_scale(keys[10], (FF,), ((0, 16),), -0.2, 0.2)), 0.5, 2.0),
        "m_up": jnp.clip(jnp.exp(math.log(2.0) - 1.3862944 * jax.random.uniform(keys[11], (FF,), jnp.float32) ** block_scale(keys[11], (FF,), ((0, 16),), -0.2, 0.2)), 0.5, 2.0),
        "m_down": jnp.clip(jnp.exp(jax.random.uniform(keys[12], (D,), jnp.float32, math.log(0.5), math.log(2.0))), 0.5, 2.0),
        "cotangent": bell_draw(keys[13], (TOKENS, D), 1.0, 6.0, ((0, 256),)),
    }


adapter_scale = 2.0
epsilon = 1e-06
highest_precision = lax.Precision.HIGHEST

def column_norm(frozen_weight, left_multiplier, right_multiplier):
    merged_weight = frozen_weight.astype(jnp.float32) + adapter_scale * jnp.dot(left_multiplier, right_multiplier, preferred_element_type=jnp.float32)
    return jnp.sqrt(lax.optimization_barrier(jnp.sum(merged_weight * merged_weight, axis=0)) + epsilon)

def silu_slope(pre_value):
    logistic = jax.nn.sigmoid(pre_value)
    return logistic * (1.0 + pre_value * (1.0 - logistic))

def low_rank(rank_output_rows, multiplier):
    return adapter_scale * jnp.dot(rank_output_rows, multiplier.astype(jnp.float32), precision=highest_precision)

def reference(inputs, gate_weight, up_weight, down_weight, gate_adapter_in, b_gate, upper_adapter_in, b_up, down_adapter_in, b_down, m_gate, m_up, m_down, cotangent):
    norm_gate = column_norm(gate_weight, gate_adapter_in, b_gate)
    norm_upper = column_norm(up_weight, upper_adapter_in, b_up)
    norm_down = column_norm(down_weight, down_adapter_in, b_down)
    gate_rank_output = jnp.dot(inputs, gate_adapter_in, preferred_element_type=jnp.float32)
    upper_rank_output = jnp.dot(inputs, upper_adapter_in, preferred_element_type=jnp.float32)
    pre_gate = jnp.dot(inputs, gate_weight, preferred_element_type=jnp.float32) + low_rank(gate_rank_output, b_gate)
    pre_upper = jnp.dot(inputs, up_weight, preferred_element_type=jnp.float32) + low_rank(upper_rank_output, b_up)
    gate_value = pre_gate * (m_gate / norm_gate)
    up_value = pre_upper * (m_up / norm_upper)
    activated = jax.nn.silu(gate_value)
    hidden_activation = (activated * up_value).astype(jnp.bfloat16)
    down_rank_output = jnp.dot(hidden_activation, down_adapter_in, preferred_element_type=jnp.float32)
    pre_down = jnp.dot(hidden_activation, down_weight, preferred_element_type=jnp.float32) + low_rank(down_rank_output, b_down)
    scale_down = m_down / norm_down
    outputs = (pre_down * scale_down).astype(jnp.bfloat16)
    grad_m_down = lax.optimization_barrier(jnp.sum(cotangent.astype(jnp.float32) * pre_down, axis=0)) / norm_down
    down_update = (cotangent.astype(jnp.float32) * scale_down).astype(jnp.bfloat16)
    down_backprop = jnp.dot(down_update, b_down.T, preferred_element_type=jnp.float32)
    down_adapter_out_gradient = adapter_scale * jnp.dot(down_rank_output.T, down_update.astype(jnp.float32), precision=highest_precision)
    down_adapter_in_gradient = adapter_scale * jnp.dot(hidden_activation.astype(jnp.float32).T, down_backprop, precision=highest_precision)
    hidden_gradient = jnp.dot(down_update, down_weight.T, preferred_element_type=jnp.float32) + adapter_scale * jnp.dot(down_backprop, down_adapter_in.astype(jnp.float32).T, precision=highest_precision)
    grad_gate = hidden_gradient * up_value * silu_slope(gate_value)
    grad_upper = hidden_gradient * activated
    grad_m_gate = lax.optimization_barrier(jnp.sum(grad_gate * pre_gate, axis=0)) / norm_gate
    grad_m_up = lax.optimization_barrier(jnp.sum(grad_upper * pre_upper, axis=0)) / norm_upper
    gate_update = (grad_gate * (m_gate / norm_gate)).astype(jnp.bfloat16)
    upper_update = (grad_upper * (m_up / norm_upper)).astype(jnp.bfloat16)
    gate_backprop = jnp.dot(gate_update, b_gate.T, preferred_element_type=jnp.float32)
    upper_backprop = jnp.dot(upper_update, b_up.T, preferred_element_type=jnp.float32)
    gate_adapter_out_gradient = adapter_scale * jnp.dot(gate_rank_output.T, gate_update.astype(jnp.float32), precision=highest_precision)
    upper_adapter_out_gradient = adapter_scale * jnp.dot(upper_rank_output.T, upper_update.astype(jnp.float32), precision=highest_precision)
    widened_inputs = inputs.astype(jnp.float32)
    gate_adapter_in_gradient = adapter_scale * jnp.dot(widened_inputs.T, gate_backprop, precision=highest_precision)
    upper_adapter_in_gradient = adapter_scale * jnp.dot(widened_inputs.T, upper_backprop, precision=highest_precision)
    input_gradient = (jnp.dot(gate_update, gate_weight.T, preferred_element_type=jnp.float32) + jnp.dot(upper_update, up_weight.T, preferred_element_type=jnp.float32) + adapter_scale * (jnp.dot(gate_backprop, gate_adapter_in.astype(jnp.float32).T, precision=highest_precision) + jnp.dot(upper_backprop, upper_adapter_in.astype(jnp.float32).T, precision=highest_precision))).astype(jnp.bfloat16)
    return (outputs, input_gradient, gate_adapter_in_gradient, upper_adapter_in_gradient, gate_adapter_out_gradient, upper_adapter_out_gradient, down_adapter_in_gradient, down_adapter_out_gradient, grad_m_gate, grad_m_up, grad_m_down)
```

```python
import jax
import jax.numpy as jnp
from jax import lax
from jax.sharding import Mesh, PartitionSpec as P

adapter_scale = 2.0
epsilon = 1e-06
bf16 = jnp.bfloat16
f32 = jnp.float32

TENSOR = ("zh", "x", "c")
DATA = ("y", "zl")
ALL = DATA + TENSOR


def swap(value, axis, distance, size):
    return lax.ppermute(value, axis, [(i, i ^ distance) for i in range(size)])


def gather_rows(own):
    pair = jnp.concatenate([own, swap(own, "zh", 1, 2)], axis=0)
    half = jnp.concatenate([pair] + [swap(pair, "x", k, 4) for k in (1, 3, 2)], axis=0)
    return jnp.concatenate([half, swap(half, "c", 1, 2)], axis=0)


def scatter_rows(partial):
    rows = partial.shape[0]
    half, away = partial[: rows // 2], partial[rows // 2 :]
    half = half.astype(f32) + swap(away.astype(bf16), "c", 1, 2).astype(f32)
    part = rows // 8
    sent = half[part:].astype(bf16)
    pair = half[:part]
    for place, k in enumerate((1, 3, 2)):
        pair = pair + swap(sent[place * part : (place + 1) * part], "x", k, 4).astype(f32)
    own = rows // 16
    return pair[:own] + swap(pair[own:].astype(bf16), "zh", 1, 2).astype(f32)


def sum_tensor(value):
    value = value + swap(value, "c", 1, 2)
    value = value + sum(swap(value, "x", k, 4) for k in (1, 3, 2))
    return value + swap(value, "zh", 1, 2)


def merge(weight, left, right):
    merged = weight.astype(f32) + adapter_scale * jnp.dot(left, right, preferred_element_type=f32)
    return merged.astype(bf16), jnp.sum(merged * merged, axis=0)


def dot_last(a, b):
    return lax.dot_general(a, b, (((1,), (1,)), ((), ())), preferred_element_type=f32)


def dot_first(a, b):
    return lax.dot_general(a, b, (((0,), (0,)), ((), ())), preferred_element_type=f32)


def pick(chunks, index):
    return lax.dynamic_index_in_dim(chunks, index, 0, keepdims=False)


def shards(
    inputs, gate_weight, up_weight, down_weight, gate_adapter_in, b_gate, upper_adapter_in, b_up,
    down_adapter_in, b_down, m_gate, m_up, m_down, cotangent,
):
    rank = gate_adapter_in.shape[1]
    features = inputs.shape[1]
    y, zl = lax.axis_index("y"), lax.axis_index("zl")

    tokens = gather_rows(inputs)
    down, down_squares = merge(down_weight, down_adapter_in, b_down)
    norm_down = jnp.sqrt(sum_tensor(down_squares) + epsilon)
    gate, gate_squares = merge(gate_weight, gate_adapter_in, b_gate)
    up, up_squares = merge(up_weight, upper_adapter_in, b_up)
    norm_gate, norm_up = jnp.sqrt(gate_squares + epsilon), jnp.sqrt(up_squares + epsilon)
    scale_gate, scale_up, scale_down = m_gate / norm_gate, m_up / norm_up, m_down / norm_down
    cot = gather_rows(cotangent)

    rank_in = jnp.dot(
        tokens, jnp.concatenate([gate_adapter_in, upper_adapter_in], axis=1), preferred_element_type=f32
    ).astype(bf16)
    pre_gate = jnp.dot(tokens, gate, preferred_element_type=f32)
    pre_up = jnp.dot(tokens, up, preferred_element_type=f32)
    gate_value, up_value = pre_gate * scale_gate, pre_up * scale_up
    logistic = jax.nn.sigmoid(gate_value)
    activated = gate_value * logistic
    hidden = (activated * up_value).astype(bf16)
    pre_down = jnp.dot(hidden, down, preferred_element_type=f32)
    rank_down = jnp.dot(hidden, down_adapter_in, preferred_element_type=f32).astype(bf16)
    outputs = (scatter_rows(pre_down) * scale_down).astype(bf16)

    cot_wide = cot.astype(f32)
    grad_m_down = jnp.sum(cot_wide * pre_down, axis=0) / norm_down
    delta_down = (cot_wide * scale_down).astype(bf16)
    back_down = dot_last(delta_down, b_down).astype(bf16)
    grad_hidden = dot_last(delta_down, down)
    grad_gate = grad_hidden * up_value * logistic * (1.0 + gate_value * (1.0 - logistic))
    grad_up = grad_hidden * activated
    grad_m_gate = jnp.sum(grad_gate * pre_gate, axis=0) / norm_gate
    grad_m_up = jnp.sum(grad_up * pre_up, axis=0) / norm_up
    delta_gate, delta_up = (grad_gate * scale_gate).astype(bf16), (grad_up * scale_up).astype(bf16)
    back = jnp.concatenate([dot_last(delta_gate, b_gate), dot_last(delta_up, b_up)], axis=1).astype(bf16)

    shared = adapter_scale * jnp.concatenate(
        [dot_first(back, tokens), dot_first(rank_down, delta_down), grad_m_down[None] / adapter_scale], axis=0
    )
    local = jnp.stack(
        [
            adapter_scale * dot_first(rank_in[:, :rank], delta_gate),
            adapter_scale * dot_first(rank_in[:, rank:], delta_up),
            adapter_scale * dot_first(back_down, hidden),
            jnp.pad(jnp.stack([grad_m_gate, grad_m_up]), ((0, rank - 2), (0, 0))),
        ]
    ).astype(bf16)

    wide = features // 4
    shared = jnp.stack([shared[:, k * wide : (k + 1) * wide] for k in range(4)])
    shared_y = pick(shared, y)
    local_y = pick(local, y).astype(f32)
    shared = shared.astype(bf16)
    for k in (1, 3, 2):
        shared_y = shared_y + swap(pick(shared, y ^ k), "y", k, 4).astype(f32)
        local_y = local_y + swap(pick(local, y ^ k), "y", k, 4).astype(f32)

    input_gradient = scatter_rows(dot_last(delta_gate, gate) + dot_last(delta_up, up)).astype(bf16)

    wide = wide // 4
    shared_y = jnp.stack([shared_y[:, k * wide : (k + 1) * wide] for k in range(4)])
    shared_z = pick(shared_y, zl)
    shared_y = shared_y.astype(bf16)
    local_sent = local_y.astype(bf16)
    for k in (1, 3, 2):
        shared_z = shared_z + swap(pick(shared_y, zl ^ k), "zl", k, 4).astype(f32)
        local_y = local_y + swap(local_sent, "zl", k, 4).astype(f32)
    local_sent = local_y.astype(bf16)
    by_distance = jnp.stack([local_sent] + [swap(local_sent, "y", k, 4) for k in (1, 2, 3)]).astype(f32)
    local_sum = [pick(by_distance, y ^ k) for k in range(4)]

    shared_sum = sum_tensor(shared_z)
    place = (lax.axis_index("zh") * 4 + lax.axis_index("x")) * 2 + lax.axis_index("c")
    mine = wide // 16
    shared_mine = lax.dynamic_slice_in_dim(shared_sum, place * mine, mine, axis=1)
    return (
        outputs,
        input_gradient,
        shared_mine[:rank].T,
        shared_mine[rank : 2 * rank].T,
        local_sum[0],
        local_sum[1],
        local_sum[2].T,
        shared_mine[2 * rank : 3 * rank],
        local_sum[3][0],
        local_sum[3][1],
        shared_mine[3 * rank],
    )


def solution(mesh):
    fine = Mesh(mesh.devices.reshape(4, 4, 2, 4, 2), ALL)
    return jax.shard_map(
        shards,
        mesh=fine,
        in_specs=(
            P(ALL, None),
            P(None, TENSOR),
            P(None, TENSOR),
            P(TENSOR, None),
            P(),
            P(None, TENSOR),
            P(),
            P(None, TENSOR),
            P(TENSOR, None),
            P(),
            P(TENSOR),
            P(TENSOR),
            P(),
            P(ALL, None),
        ),
        out_specs=(
            P(ALL, None),
            P(ALL, None),
            P(ALL, None),
            P(ALL, None),
            P(None, TENSOR),
            P(None, TENSOR),
            P(TENSOR, None),
            P(None, ALL),
            P(TENSOR),
            P(TENSOR),
            P(ALL),
        ),
        check_vma=False,
    )
```

```python
import jax
import jax.numpy as jnp
from jax import lax
from jax.experimental import pallas as pl
from jax.experimental.pallas import tpu as pltpu
from jax.sharding import Mesh, PartitionSpec as P

adapter_scale = 2.0
epsilon = 1e-06
bf16 = jnp.bfloat16
f32 = jnp.float32

DATA = ("y", "zl")
TENSOR = ("zh", "x", "c")
ALL = DATA + TENSOR
X_ORDER = (1, 3, 2)
MIB = 1024 * 1024
ANY = pl.BlockSpec(memory_space=pl.ANY)
VMEM = pl.BlockSpec(memory_space=pltpu.VMEM)
SMEM = pl.BlockSpec(memory_space=pltpu.SMEM)
SPANS = ((0, 256), (256, 256), (512, 288))
WIDE = 640
RANK = 32
SHARED = 64


def swap(value, axis, distance, size):
    return lax.ppermute(value, axis, [(i, i ^ distance) for i in range(size)])


def swap_core(value):
    return swap(value, "c", 1, 2)


def swap_z(value):
    return swap(value, ("zl", "zh"), 5, 8)


def swap_x(value):
    return [swap(value, "x", k, 4) for k in X_ORDER]


def dot(a, b):
    return jnp.dot(a, b, preferred_element_type=f32)


def dot_last(a, b):
    return lax.dot_general(a, b, (((1,), (1,)), ((), ())), preferred_element_type=f32)


def dot_first(a, b):
    return lax.dot_general(a, b, (((0,), (0,)), ((), ())), preferred_element_type=f32)


def shape(*dims, dtype=bf16):
    return jax.ShapeDtypeStruct(dims, dtype)


def call(kernel, name, out_shape, mib, flops=1000, **kwargs):
    return pl.pallas_call(
        kernel,
        out_shape=out_shape,
        compiler_params=pltpu.CompilerParams(vmem_limit_bytes=mib * MIB),
        cost_estimate=pl.CostEstimate(flops=flops, bytes_accessed=1000, transcendentals=0),
        name=name,
        **kwargs,
    )


def parts(features):
    return [pl.ds(i, WIDE) for i in range(0, features, WIDE)]


def down_squares_kernel(w_ref, a_ref, b_ref, squares_ref):
    for part in parts(w_ref.shape[1]):
        merged = w_ref[:, part].astype(f32) + adapter_scale * dot_first(a_ref[...], b_ref[:, part])
        squares_ref[:, part] = jnp.sum(merged * merged, axis=0, keepdims=True)


def down_squares(weight, left_t, right):
    return call(
        down_squares_kernel,
        "down_squares",
        shape(1, weight.shape[1], dtype=f32),
        6,
        in_specs=[VMEM] * 3,
        out_specs=VMEM,
    )(weight, left_t, right)


class Copies:
    def __init__(self, pairs, sems, ahead):
        self.copies = [pltpu.make_async_copy(a, b, sems.at[i]) for i, (a, b) in enumerate(pairs)]
        self.started = self.waited = 0
        self.ahead = ahead
        self.fill()

    def fill(self):
        while self.started < min(len(self.copies), self.waited + self.ahead):
            self.copies[self.started].start()
            self.started += 1

    def wait(self):
        self.copies[self.waited].wait()
        self.waited += 1
        self.fill()


def merge_kernel(
    after, g_ref, u_ref, d_ref, ga, ua, gb, ub, ad, bd, g_m, u_m, g_out, u_out, d_out, g_scale, u_scale,
    g_held, u_held, d_held, sems,
):
    spans = parts(g_ref.shape[1])
    pairs = []
    for ref, held in ((g_ref, g_held), (u_ref, u_held), (d_ref, d_held)):
        pairs += [(ref.at[:, part], held.at[:, part]) for part in spans]
    copies = Copies(pairs, sems, 6)
    for w, a, b, m, out, scale in ((g_held, ga, gb, g_m, g_out, g_scale), (u_held, ua, ub, u_m, u_out, u_scale)):
        squares = 0.0
        for part in spans:
            copies.wait()
            merged = w[:, part].astype(f32) + adapter_scale * dot_first(b[...], a[:, part])
            out[:, part] = merged.astype(bf16)
            square = merged * merged
            squares += sum(square[:, k : k + 128] for k in range(0, WIDE, 128))
        total = jnp.sum(jnp.transpose(squares), axis=0, keepdims=True)
        scale[...] = m[...] / jnp.sqrt(total + epsilon)
    for part in spans:
        copies.wait()
        merged = d_held[:, part].astype(f32) + adapter_scale * dot_first(ad[...], bd[:, part])
        d_out[:, part] = merged.astype(bf16)


def merge(after, gate, up, down, *others):
    units, features = gate.shape
    return call(
        merge_kernel,
        "merge",
        [shape(*gate.shape)] * 3 + [shape(1, units, dtype=f32)] * 2,
        40,
        in_specs=[ANY] * 4 + [VMEM] * len(others),
        out_specs=[VMEM] * 5,
        scratch_shapes=[pltpu.VMEM(gate.shape, bf16)] * 3 + [pltpu.SemaphoreType.DMA((3 * (features // WIDE),))],
    )(after, gate, up, down, *others)


def forward_kernel(
    after, mine, away, gate, up, down, ga_t, ua_t, ad_t, g_scale, u_scale,
    p_mine, p_away, hidden_out, gate_out, up_out, rank_in_t, rank_down_t, rows,
):
    half = mine.shape[0]
    rows[:half] = mine[...]
    rows[half:] = away[...]
    rank_down = 0.0
    for start, size in SPANS:
        span = pl.ds(start, size)
        gate_value = dot_last(rows[...], gate[span, :]) * g_scale[:, span]
        up_value = dot_last(rows[...], up[span, :]) * u_scale[:, span]
        gate_out[:, span] = gate_value.astype(bf16)
        up_out[:, span] = up_value.astype(bf16)
        hidden = (gate_value * jax.nn.sigmoid(gate_value) * up_value).astype(bf16)
        hidden_out[:, span] = hidden
        rank_down += dot_last(ad_t[:, span], hidden)
    rank_down_t[...] = rank_down.astype(bf16)
    for part in parts(down.shape[1]):
        p = dot(hidden_out[...], down[:, part]).astype(bf16)
        p_mine[:, part] = p[:half]
        p_away[:, part] = p[half:]
    rank_in_t[:RANK, :] = dot_last(ga_t[...], rows[...]).astype(bf16)
    rank_in_t[RANK:, :] = dot_last(ua_t[...], rows[...]).astype(bf16)


def forward(after, mine, *others):
    half, features = mine.shape
    units = others[1].shape[0]
    return call(
        forward_kernel,
        "forward",
        [shape(half, features)] * 2 + [shape(2 * half, units)] * 3 + [shape(2 * RANK, 2 * half), shape(RANK, 2 * half)],
        6,
        in_specs=[ANY] + [VMEM] * (1 + len(others)),
        out_specs=[VMEM] * 7,
        scratch_shapes=[pltpu.VMEM((2 * half, features), bf16)],
    )(after, mine, *others)


def backward_kernel(
    y, core, cot_mine, cot_away, mine, away, p_mine, p_away, down, hidden, gate_value, up_value,
    rank_in_t, rank_down_t, b_down, b_gate, b_up, g_scale, u_scale, m_gate, m_up, d_sq, m_down,
    delta_gate_out, delta_up_out, shared_own, shared_away, local_out,
    delta, local,
):
    units, features = down.shape
    half = mine.shape[0]
    block = features // 4
    norm_down = jnp.sqrt(d_sq[...] + epsilon)
    scale_down = m_down[...] / norm_down
    delta[:half] = (cot_mine[...].astype(f32) * scale_down).astype(bf16)
    delta[half:] = (cot_away[...].astype(f32) * scale_down).astype(bf16)
    back_down_t = dot_last(b_down[...], delta[...]).astype(bf16)
    back_gate = back_up = 0.0
    local[:, :, pl.ds(768, 512)] = jnp.zeros((4, RANK, 512), bf16)
    for start, size in SPANS:
        span = pl.ds(start, size)
        grad_hidden = dot_last(delta[...], down[span, :])
        gate = gate_value[:, span].astype(f32)
        upper = up_value[:, span].astype(f32)
        logistic = jax.nn.sigmoid(gate)
        activated = gate * logistic
        grad_up = grad_hidden * activated
        grad_gate = grad_hidden * upper * (logistic + activated * (1.0 - logistic))
        grad_m_gate = jnp.sum(grad_gate * gate, axis=0, keepdims=True) / m_gate[:, span]
        grad_m_up = jnp.sum(grad_up * upper, axis=0, keepdims=True) / m_up[:, span]
        delta_gate = (grad_gate * g_scale[:, span]).astype(bf16)
        delta_up = (grad_up * u_scale[:, span]).astype(bf16)
        delta_gate_out[:, span] = delta_gate
        delta_up_out[:, span] = delta_up
        back_gate += dot_last(b_gate[:, span], delta_gate)
        back_up += dot_last(b_up[:, span], delta_up)
        local[0, :, span] = (adapter_scale * dot(rank_in_t[:RANK, :], delta_gate)).astype(bf16)
        local[1, :, span] = (adapter_scale * dot(rank_in_t[RANK:, :], delta_up)).astype(bf16)
        local[2, :, span] = (adapter_scale * dot(back_down_t, hidden[:, span])).astype(bf16)
        stats = jnp.concatenate([grad_m_gate, grad_m_up, jnp.zeros((RANK - 2, size), f32)], axis=0)
        local[3, :, span] = stats.astype(bf16)
    back_t = jnp.concatenate([back_gate, back_up], axis=0).astype(bf16)
    here = y[0]
    first = core[0] == 0
    for k in range(4):
        chunk = here ^ k
        part = pl.ds(pl.multiple_of(chunk * block, 128), block)
        own = local[chunk]
        folded = sum(
            pltpu.roll(own[i * 8 : (i + 1) * 8, block:].astype(f32), i * (units - block), 1) for i in range(4)
        )
        local_out[k, pl.ds(0, RANK), :] = own[:, :block]
        folded = jnp.concatenate([folded, jnp.zeros((8, block), f32)], axis=0)
        local_out[k, pl.ds(RANK, 16), :] = folded.astype(bf16)
        back_rows = adapter_scale * (dot(back_t[:, :half], mine[:, part]) + dot(back_t[:, half:], away[:, part]))
        down_rows = adapter_scale * dot(rank_down_t[...], delta[:, part])
        moment = sum(
            jnp.sum(cot[:, part].astype(f32) * partial[:, part].astype(f32), axis=0, keepdims=True)
            for cot, partial in ((cot_mine, p_mine), (cot_away, p_away))
        )
        moment = moment / jnp.sqrt(d_sq[:, part] + epsilon)
        zeros = jnp.zeros((15, block), f32)
        one = jnp.concatenate([back_rows[:RANK], down_rows[:16], jnp.zeros((16, block), f32)], axis=0)
        two = jnp.concatenate([back_rows[RANK:], down_rows[16:], moment, zeros], axis=0)
        shared_own[k] = jnp.where(first, one, two).astype(bf16)
        shared_away[k] = jnp.where(first, two, one).astype(bf16)


def backward(y, core, *others):
    half, features = others[0].shape
    units = others[6].shape[0]
    return call(
        backward_kernel,
        "backward",
        [shape(2 * half, units)] * 2 + [shape(4, SHARED, features // 4)] * 2 + [shape(4, RANK + 16, features // 4)],
        10,
        in_specs=[SMEM] * 2 + [VMEM] * len(others),
        out_specs=[VMEM] * 5,
        scratch_shapes=[pltpu.VMEM((2 * half, features), bf16), pltpu.VMEM((4, RANK, 2 * (features // 4)), bf16)],
    )(y, core, *others)


def input_gradient_kernel(delta_gate, delta_up, gate, up, mine, away):
    half = mine.shape[0]
    for part in parts(gate.shape[1]):
        total = dot(delta_gate[...], gate[:, part]) + dot(delta_up[...], up[:, part])
        total = total.astype(bf16)
        mine[:, part] = total[:half]
        away[:, part] = total[half:]


def input_gradient_of(delta_gate, delta_up, gate, up):
    rows = delta_gate.shape[0] // 2
    return call(
        input_gradient_kernel,
        "input_gradient",
        [shape(rows, gate.shape[1])] * 2,
        5,
        flops=8 * rows * gate.size,
        in_specs=[VMEM] * 4,
        out_specs=[VMEM, VMEM],
    )(delta_gate, delta_up, gate, up)


def core_sum_kernel(after, own, got, local, out0, out1, out2, out3):
    for k, out in enumerate((out0, out1, out2, out3)):
        total = own[k].astype(f32) + got[k].astype(f32)
        folded = local[k, pl.ds(RANK, 16), :].astype(f32)
        out[pl.ds(0, SHARED), :] = jnp.concatenate([total[: SHARED - 8], folded[:8]], axis=0).astype(bf16)
        out[pl.ds(SHARED, RANK), :] = local[k, pl.ds(0, RANK), :]


def core_sum(after, own, got, local):
    return call(
        core_sum_kernel,
        "core_sum",
        [shape(SHARED + RANK, own.shape[2])] * 4,
        4,
        in_specs=[ANY] + [VMEM] * 3,
        out_specs=[VMEM] * 4,
    )(after, own, got, local)


def after_y_kernel(zl, after, own, a, b, c, out0, out1, out2, out3, shared):
    total = own[...].astype(f32) + a[...].astype(f32) + b[...].astype(f32) + c[...].astype(f32)
    wide = out0.shape[1]
    quarter = total.shape[1] // 4
    here = zl[0]
    for j in range(4):
        shared[j, :, pl.ds(0, quarter)] = total[:SHARED, j * quarter : (j + 1) * quarter]
    folded = total[SHARED - 8 : SHARED]
    rest = jnp.concatenate([folded[:, i * quarter : (i + 1) * quarter] for i in range(4)], axis=0)
    local = jnp.concatenate([total[SHARED:], rest], axis=1).astype(bf16)
    for k, out in enumerate((out0, out1, out2, out3)):
        out[pl.ds(0, SHARED), :] = shared[here ^ k].astype(bf16)
        for i in range(3):
            out[pl.ds(SHARED + i * RANK, RANK), :] = local[:, i * wide : (i + 1) * wide]
        out[pl.ds(SHARED + 3 * RANK, RANK), pl.ds(0, local.shape[1] - 3 * wide)] = local[:, 3 * wide :]


def after_y(zl, after, own, others):
    return call(
        after_y_kernel,
        "after_y",
        [shape(SHARED + 4 * RANK, 256)] * 4,
        4,
        in_specs=[SMEM, ANY] + [VMEM] * 4,
        out_specs=[VMEM] * 4,
        scratch_shapes=[pltpu.VMEM((4, SHARED, 256), f32)],
    )(zl, after, own, *others)


def after_z_kernel(own, a, b, c, shared, local):
    total = own[...].astype(f32) + a[...].astype(f32) + b[...].astype(f32) + c[...].astype(f32)
    shared[...] = total[:SHARED, : shared.shape[1]]
    wide = own.shape[1]
    for i in range(4):
        width = min(wide, local.shape[1] - i * wide)
        first = SHARED + i * RANK
        local[:, pl.ds(i * wide, width)] = total[first : first + RANK, :width].astype(bf16)


def after_z(own, others, quarter, units):
    return call(
        after_z_kernel,
        "after_z",
        [shape(SHARED, quarter, dtype=f32), shape(RANK, units)],
        4,
        in_specs=[VMEM] * 4,
        out_specs=[VMEM] * 2,
    )(own, *others)


def x_sum_kernel(own, a, b, c, local, out, sent, local_out):
    total = own[...] + a[...].astype(f32) + b[...].astype(f32) + c[...].astype(f32)
    out[...] = total
    sent[...] = total.astype(bf16)
    local_out[...] = local[...]


def x_sum(own, others, local):
    return call(
        x_sum_kernel,
        "x_sum",
        [shape(*own.shape, dtype=f32), shape(*own.shape), shape(*local.shape)],
        4,
        in_specs=[VMEM] * 5,
        out_specs=[VMEM] * 3,
    )(own, *others, local)


def local_out_kernel(y, own, a, b, c, gate, up, down, stats, held):
    for k, piece in enumerate((own, a, b, c)):
        held[k] = piece[...]
    here = y[0]
    for j, out in enumerate((gate, up, down)):
        out[...] = held[here ^ j].astype(f32)
    stats[...] = held[here ^ 3][:8].astype(f32)


def local_out(y, own, others):
    units = own.shape[1]
    return call(
        local_out_kernel,
        "local_out",
        [shape(RANK, units, dtype=f32)] * 3 + [shape(8, units, dtype=f32)],
        4,
        in_specs=[SMEM] + [VMEM] * 4,
        out_specs=[VMEM] * 4,
        scratch_shapes=[pltpu.VMEM((4, RANK, units), bf16)],
    )(y, own, *others)


def shared_out_kernel(place, core, own, got, gate, up, down, moment):
    wide = gate.shape[0]
    first = core[0] == 0
    halves = jnp.where(first, own[...], got[...]), jnp.where(first, got[...], own[...])
    spots = (16, own.shape[1])
    row = lax.broadcasted_iota(jnp.int32, spots, 0)
    chosen = (lax.broadcasted_iota(jnp.int32, spots, 1) == place[0] * wide + row).astype(f32)
    highest = lax.Precision.HIGHEST
    last = (((1,), (1,)), ((), ()))
    one, two = [lax.dot_general(chosen, h, last, precision=highest, preferred_element_type=f32) for h in halves]
    gate[...] = one[:wide, :RANK]
    up[...] = two[:wide, :RANK]
    down[:, pl.ds(0, 16)] = one[:wide, RANK : RANK + 16]
    down[:, pl.ds(16, 16)] = two[:wide, RANK : RANK + 16]
    line = lax.dot_general(halves[1][48:56], chosen, last, precision=highest, preferred_element_type=f32)
    moment[...] = line[:1, :wide]


def shared_out(place, core, own, got):
    wide = own.shape[1] // 16
    return call(
        shared_out_kernel,
        "shared_out",
        [shape(wide, RANK, dtype=f32)] * 3 + [shape(1, wide, dtype=f32)],
        4,
        in_specs=[SMEM] * 2 + [VMEM] * 2,
        out_specs=[VMEM] * 4,
    )(place, core, own, got)


def half_sum_kernel(p_mine, p_got, i_mine, i_got, pair, one, two, three):
    part = p_mine.shape[0] // 4
    for place, mine, got in ((0, p_mine, p_got), (part, i_mine, i_got)):
        rows = pl.ds(place, part)
        total = mine[...].astype(f32) + got[...].astype(f32)
        pair[rows, :] = total[:part]
        for i, out in enumerate((one, two, three)):
            out[rows, :] = total[(i + 1) * part : (i + 2) * part].astype(bf16)


def half_sum(p_mine, p_got, i_mine, i_got):
    rows, features = p_mine.shape
    part = rows // 2
    return call(
        half_sum_kernel,
        "half_sum",
        [shape(part, features, dtype=f32)] + [shape(part, features)] * 3,
        5,
        in_specs=[VMEM] * 4,
        out_specs=[VMEM] * 4,
    )(p_mine, p_got, i_mine, i_got)


def pair_sum_kernel(pair, a, b, c, own, sent):
    total = pair[...] + a[...].astype(f32) + b[...].astype(f32) + c[...].astype(f32)
    rows = total.shape[0] // 4
    for i in range(2):
        first = 2 * i * rows
        own[pl.ds(i * rows, rows), :] = total[first : first + rows]
        sent[pl.ds(i * rows, rows), :] = total[first + rows : first + 2 * rows].astype(bf16)


def pair_sum(pair, got):
    rows, features = pair.shape
    return call(
        pair_sum_kernel,
        "pair_sum",
        [shape(rows // 2, features, dtype=f32), shape(rows // 2, features)],
        4,
        in_specs=[VMEM] * 4,
        out_specs=[VMEM] * 2,
    )(pair, *got)


def rows_out_kernel(own, got, d_sq, m_down, outputs, input_gradient):
    rows = outputs.shape[0]
    total = own[...] + got[...].astype(f32)
    scale_down = m_down[...] / jnp.sqrt(d_sq[...] + epsilon)
    outputs[...] = (total[:rows] * scale_down).astype(bf16)
    input_gradient[...] = total[rows:].astype(bf16)


def rows_out(own, got, d_sq, m_down):
    rows, features = own.shape
    return call(
        rows_out_kernel,
        "rows_out",
        [shape(rows // 2, features)] * 2,
        4,
        in_specs=[VMEM] * 4,
        out_specs=[VMEM] * 2,
    )(own, got, d_sq, m_down)


def held_until_kernel(after, value, out):
    out[...] = value[...]


def held_until(after, value):
    return call(
        held_until_kernel,
        "held_until",
        shape(*value.shape, dtype=value.dtype),
        2,
        in_specs=[ANY, VMEM],
        out_specs=VMEM,
    )(after, value)


def split(value):
    high = value.astype(bf16)
    return jnp.concatenate([high, (value - high.astype(f32)).astype(bf16)], axis=0)


def joined(rows):
    return rows[0:1].astype(f32) + rows[1:2].astype(f32)


def shards(
    inputs, gate_weight, up_weight, down_weight, gate_adapter_in, b_gate, upper_adapter_in, b_up,
    down_adapter_in, b_down, m_gate, m_up, m_down, cotangent,
):
    rows, features = inputs.shape
    units = down_weight.shape[0]
    y, zl, core = lax.axis_index("y")[None], lax.axis_index("zl")[None], lax.axis_index("c")[None]
    place = (lax.axis_index("zh") * 4 + lax.axis_index("x")) * 2 + lax.axis_index("c")
    m_gate, m_up, m_down = m_gate[None], m_up[None], m_down[None]
    gate_t, up_t = gate_weight.T, up_weight.T
    ga_t, ua_t, ad_t = gate_adapter_in.T, upper_adapter_in.T, down_adapter_in.T

    other = swap_z(inputs)
    squares = held_until(other, down_squares(down_weight, ad_t, b_down))
    got = swap_z(jnp.concatenate([cotangent, split(squares)], axis=0))
    pair = jnp.concatenate([inputs, other], axis=0)
    got_x = swap_x(pair)
    mine = jnp.concatenate([pair] + got_x, axis=0)
    squares = squares + joined(got[rows:])
    pair = jnp.concatenate([cotangent, got[:rows]], axis=0)
    got = swap_x(jnp.concatenate([pair, split(squares)], axis=0))

    gate, up, down, g_scale, u_scale = merge(
        got_x[0], gate_t, up_t, down_weight, ga_t, ua_t, b_gate, b_up, ad_t, b_down, m_gate, m_up
    )
    away = swap_core(mine)
    cot_mine = jnp.concatenate([pair] + [g[: 2 * rows] for g in got], axis=0)
    cot_away = swap_core(cot_mine)
    squares = squares + sum(joined(g[2 * rows :]) for g in got)
    squares = squares + swap_core(squares)

    p_mine, p_away, hidden, gate_value, up_value, rank_in_t, rank_down_t = forward(
        cot_mine, mine, away, gate, up, down, ga_t, ua_t, ad_t, g_scale, u_scale
    )
    p_got = swap_core(p_away)

    delta_gate, delta_up, shared_own, shared_away, local = backward(
        y, core, cot_mine, cot_away, mine, away, p_mine, p_away, down, hidden, gate_value, up_value,
        rank_in_t, rank_down_t, b_down, b_gate, b_up, g_scale, u_scale, m_gate, m_up, squares, m_down,
    )
    i_mine, i_away = input_gradient_of(delta_gate, delta_up, gate, up)
    packed = core_sum(i_mine, shared_own, swap_core(shared_away), local)
    pair, *sent = half_sum(p_mine, p_got, i_mine, swap_core(i_away))
    own, *sent_z = after_y(zl, pair, packed[0], [swap(packed[k], "y", k, 4) for k in (1, 2, 3)])

    quarter = features // 16
    shared, local = after_z(own, [swap(v, "zl", k + 1, 4) for k, v in enumerate(sent_z)], quarter, units)
    shared, sent_zh, local = x_sum(shared, swap_x(shared.astype(bf16)), local)
    shared = shared + swap(sent_zh, "zh", 1, 2).astype(f32)
    gate_in, up_in, down_in, moment = shared_out(place[None], core, shared, swap_core(shared))
    gate_out, up_out, down_out, stats = local_out(y, local, [swap(local, "y", k, 4) for k in (1, 2, 3)])

    own, sent = pair_sum(pair, [swap(v, "x", k, 4) for k, v in zip(X_ORDER, sent)])
    outputs, input_gradient = rows_out(own, swap_z(sent), squares, m_down)

    return (
        outputs,
        input_gradient,
        gate_in,
        up_in,
        gate_out,
        up_out,
        down_out.T,
        down_in.T,
        stats[0],
        stats[1],
        moment[0],
    )


def solution(mesh):
    fine = Mesh(mesh.devices.reshape(4, 4, 2, 4, 2), ALL)
    return jax.shard_map(
        shards,
        mesh=fine,
        in_specs=(
            P(ALL, None),
            P(None, TENSOR),
            P(None, TENSOR),
            P(TENSOR, None),
            P(),
            P(None, TENSOR),
            P(),
            P(None, TENSOR),
            P(TENSOR, None),
            P(),
            P(TENSOR),
            P(TENSOR),
            P(),
            P(ALL, None),
        ),
        out_specs=(
            P(ALL, None),
            P(ALL, None),
            P(ALL, None),
            P(ALL, None),
            P(None, TENSOR),
            P(None, TENSOR),
            P(TENSOR, None),
            P(None, ALL),
            P(TENSOR),
            P(TENSOR),
            P(ALL),
        ),
        check_vma=False,
    )
```

```python
import jax
import jax.numpy as jnp
from jax import lax
from jax.experimental import pallas as pl
from jax.experimental.pallas import tpu as pltpu
from jax.sharding import Mesh, PartitionSpec as P

adapter_scale = 2.0
epsilon = 1e-06
bf16 = jnp.bfloat16
f32 = jnp.float32

DATA = ("y", "zl")
TENSOR = ("zh", "x", "c")
ALL = DATA + TENSOR
X_ORDER = (1, 3, 2)
MIB = 1024 * 1024
ANY = pl.BlockSpec(memory_space=pl.ANY)
VMEM = pl.BlockSpec(memory_space=pltpu.VMEM)
SMEM = pl.BlockSpec(memory_space=pltpu.SMEM)
SPANS = ((0, 256), (256, 256), (512, 288))
WIDE = 640
RANK = 32
SHARED = 64


def swap(value, axis, distance, size):
    return lax.ppermute(value, axis, [(i, i ^ distance) for i in range(size)])


def swap_core(value):
    return swap(value, "c", 1, 2)


def swap_z(value):
    return swap(value, ("zl", "zh"), 5, 8)


def swap_x(value):
    return [swap(value, "x", k, 4) for k in X_ORDER]


def dot(a, b):
    return jnp.dot(a, b, preferred_element_type=f32)


def dot_last(a, b):
    return lax.dot_general(a, b, (((1,), (1,)), ((), ())), preferred_element_type=f32)


def dot_first(a, b):
    return lax.dot_general(a, b, (((0,), (0,)), ((), ())), preferred_element_type=f32)


def shape(*dims, dtype=bf16):
    return jax.ShapeDtypeStruct(dims, dtype)


def call(kernel, name, out_shape, mib, flops=1000, **kwargs):
    return pl.pallas_call(
        kernel,
        out_shape=out_shape,
        compiler_params=pltpu.CompilerParams(vmem_limit_bytes=mib * MIB),
        cost_estimate=pl.CostEstimate(flops=flops, bytes_accessed=1000, transcendentals=0),
        name=name,
        **kwargs,
    )


def parts(features):
    return [pl.ds(i, WIDE) for i in range(0, features, WIDE)]


class Copies:
    def __init__(self, pairs, sems, ahead):
        self.copies = [pltpu.make_async_copy(a, b, sems.at[i]) for i, (a, b) in enumerate(pairs)]
        self.started = self.waited = 0
        self.ahead = ahead
        self.fill()

    def fill(self):
        while self.started < min(len(self.copies), self.waited + self.ahead):
            self.copies[self.started].start()
            self.started += 1

    def wait(self):
        self.copies[self.waited].wait()
        self.waited += 1
        self.fill()


def down_squares_kernel(w_ref, a_ref, b_ref, squares_ref, w, a, b, sems):
    spans = parts(w_ref.shape[1])
    pairs = [(a_ref, a), (b_ref, b)] + [(w_ref.at[:, part], w.at[:, part]) for part in spans]
    copies = Copies(pairs, sems, len(pairs))
    copies.wait()
    copies.wait()
    for part in spans:
        copies.wait()
        merged = w[:, part].astype(f32) + adapter_scale * dot_first(a[...], b[:, part])
        squares_ref[:, part] = jnp.sum(merged * merged, axis=0, keepdims=True)


def down_squares(weight, left_t, right):
    return call(
        down_squares_kernel,
        "down_squares",
        shape(1, weight.shape[1], dtype=f32),
        56,
        in_specs=[ANY] * 3,
        out_specs=VMEM,
        scratch_shapes=[
            pltpu.VMEM(weight.shape, bf16),
            pltpu.VMEM(left_t.shape, bf16),
            pltpu.VMEM(right.shape, bf16),
            pltpu.SemaphoreType.DMA((2 + weight.shape[1] // WIDE,)),
        ],
    )(weight, left_t, right)


def merge_kernel(
    after, g_ref, u_ref, d_ref, ga, ua, gb, ub, ad, bd, g_m, u_m, g_out, u_out, d_out, g_scale, u_scale,
    g_held, u_held, d_held, sems,
):
    spans = parts(g_ref.shape[1])
    pairs = []
    for part in (pl.ds(0, 2 * WIDE), pl.ds(2 * WIDE, 2 * WIDE)):
        pairs.append((g_ref.at[:, part], g_held.at[:, part]))
    pairs += [(u_ref, u_held), (d_ref, d_held)]
    copies = Copies(pairs, sems, len(pairs))
    for w, a, b, m, out, scale in ((g_held, ga, gb, g_m, g_out, g_scale), (u_held, ua, ub, u_m, u_out, u_scale)):
        squares = 0.0
        for n, part in enumerate(spans):
            if n == 0 or (n == 2 and w is g_held):
                copies.wait()
            merged = w[:, part].astype(f32) + adapter_scale * dot_first(b[...], a[:, part])
            out[:, part] = merged.astype(bf16)
            square = merged * merged
            squares += sum(square[:, k : k + 128] for k in range(0, WIDE, 128))
        total = jnp.sum(jnp.transpose(squares), axis=0, keepdims=True)
        scale[...] = m[...] / jnp.sqrt(total + epsilon)
    copies.wait()
    for part in spans:
        merged = d_held[:, part].astype(f32) + adapter_scale * dot_first(ad[...], bd[:, part])
        d_out[:, part] = merged.astype(bf16)


def merge(after, gate, up, down, *others):
    units, features = gate.shape
    return call(
        merge_kernel,
        "merge",
        [shape(*gate.shape)] * 3 + [shape(1, units, dtype=f32)] * 2,
        40,
        in_specs=[ANY] * 4 + [VMEM] * len(others),
        out_specs=[VMEM] * 5,
        scratch_shapes=[pltpu.VMEM(gate.shape, bf16)] * 3 + [pltpu.SemaphoreType.DMA((4,))],
    )(after, gate, up, down, *others)


def forward_kernel(
    after, mine, away, gate, up, down, ga_t, ua_t, ad_t, g_scale, u_scale,
    p_mine, p_away, hidden_out, gate_out, up_out, rank_in_t, rank_down_t, rows,
):
    half = mine.shape[0]
    rows[:half] = mine[...]
    rows[half:] = away[...]
    rank_down = 0.0
    for start, size in SPANS:
        span = pl.ds(start, size)
        gate_value = dot_last(rows[...], gate[span, :]) * g_scale[:, span]
        up_value = dot_last(rows[...], up[span, :]) * u_scale[:, span]
        gate_out[:, span] = gate_value.astype(bf16)
        up_out[:, span] = up_value.astype(bf16)
        hidden = (gate_value * jax.nn.sigmoid(gate_value) * up_value).astype(bf16)
        hidden_out[:, span] = hidden
        rank_down += dot_last(ad_t[:, span], hidden)
    rank_down_t[...] = rank_down.astype(bf16)
    for part in parts(down.shape[1]):
        p = dot(hidden_out[...], down[:, part]).astype(bf16)
        p_mine[:, part] = p[:half]
        p_away[:, part] = p[half:]
    rank_in_t[:RANK, :] = dot_last(ga_t[...], rows[...]).astype(bf16)
    rank_in_t[RANK:, :] = dot_last(ua_t[...], rows[...]).astype(bf16)


def forward(after, mine, *others):
    half, features = mine.shape
    units = others[1].shape[0]
    return call(
        forward_kernel,
        "forward",
        [shape(half, features)] * 2 + [shape(2 * half, units)] * 3 + [shape(2 * RANK, 2 * half), shape(RANK, 2 * half)],
        6,
        in_specs=[ANY] + [VMEM] * (1 + len(others)),
        out_specs=[VMEM] * 7,
        scratch_shapes=[pltpu.VMEM((2 * half, features), bf16)],
    )(after, mine, *others)


def backward_kernel(
    y, core, cot_mine, cot_away, mine, away, p_mine, p_away, down, hidden, gate_value, up_value,
    rank_in_t, rank_down_t, b_down, b_gate, b_up, g_scale, u_scale, m_gate, m_up, d_sq, m_down,
    delta_gate_out, delta_up_out, shared_own, shared_away, local_out,
    delta, local,
):
    units, features = down.shape
    half = mine.shape[0]
    block = features // 4
    norm_down = jnp.sqrt(d_sq[...] + epsilon)
    scale_down = m_down[...] / norm_down
    delta[:half] = (cot_mine[...].astype(f32) * scale_down).astype(bf16)
    delta[half:] = (cot_away[...].astype(f32) * scale_down).astype(bf16)
    back_down_t = dot_last(b_down[...], delta[...]).astype(bf16)
    back_gate = back_up = 0.0
    local[:, :, pl.ds(768, 512)] = jnp.zeros((4, RANK, 512), bf16)
    for start, size in SPANS:
        span = pl.ds(start, size)
        grad_hidden = dot_last(delta[...], down[span, :])
        gate = gate_value[:, span].astype(f32)
        upper = up_value[:, span].astype(f32)
        logistic = jax.nn.sigmoid(gate)
        activated = gate * logistic
        grad_up = grad_hidden * activated
        grad_gate = grad_hidden * upper * (logistic + activated * (1.0 - logistic))
        grad_m_gate = jnp.sum(grad_gate * gate, axis=0, keepdims=True) / m_gate[:, span]
        grad_m_up = jnp.sum(grad_up * upper, axis=0, keepdims=True) / m_up[:, span]
        delta_gate = (grad_gate * g_scale[:, span]).astype(bf16)
        delta_up = (grad_up * u_scale[:, span]).astype(bf16)
        delta_gate_out[:, span] = delta_gate
        delta_up_out[:, span] = delta_up
        back_gate += dot_last(b_gate[:, span], delta_gate)
        back_up += dot_last(b_up[:, span], delta_up)
        local[0, :, span] = (adapter_scale * dot(rank_in_t[:RANK, :], delta_gate)).astype(bf16)
        local[1, :, span] = (adapter_scale * dot(rank_in_t[RANK:, :], delta_up)).astype(bf16)
        local[2, :, span] = (adapter_scale * dot(back_down_t, hidden[:, span])).astype(bf16)
        stats = jnp.concatenate([grad_m_gate, grad_m_up, jnp.zeros((RANK - 2, size), f32)], axis=0)
        local[3, :, span] = stats.astype(bf16)
    back_t = jnp.concatenate([back_gate, back_up], axis=0).astype(bf16)
    here = y[0]
    first = core[0] == 0
    for k in range(4):
        chunk = here ^ k
        part = pl.ds(pl.multiple_of(chunk * block, 128), block)
        own = local[chunk]
        folded = sum(
            pltpu.roll(own[i * 8 : (i + 1) * 8, block:].astype(f32), i * (units - block), 1) for i in range(4)
        )
        local_out[k, pl.ds(0, RANK), :] = own[:, :block]
        folded = jnp.concatenate([folded, jnp.zeros((8, block), f32)], axis=0)
        local_out[k, pl.ds(RANK, 16), :] = folded.astype(bf16)
        back_rows = adapter_scale * (dot(back_t[:, :half], mine[:, part]) + dot(back_t[:, half:], away[:, part]))
        down_rows = adapter_scale * dot(rank_down_t[...], delta[:, part])
        moment = sum(
            jnp.sum(cot[:, part].astype(f32) * partial[:, part].astype(f32), axis=0, keepdims=True)
            for cot, partial in ((cot_mine, p_mine), (cot_away, p_away))
        )
        moment = moment / jnp.sqrt(d_sq[:, part] + epsilon)
        zeros = jnp.zeros((15, block), f32)
        one = jnp.concatenate([back_rows[:RANK], down_rows[:16], jnp.zeros((16, block), f32)], axis=0)
        two = jnp.concatenate([back_rows[RANK:], down_rows[16:], moment, zeros], axis=0)
        shared_own[k] = jnp.where(first, one, two).astype(bf16)
        shared_away[k] = jnp.where(first, two, one).astype(bf16)


def backward(y, core, *others):
    half, features = others[0].shape
    units = others[6].shape[0]
    return call(
        backward_kernel,
        "backward",
        [shape(2 * half, units)] * 2 + [shape(4, SHARED, features // 4)] * 2 + [shape(4, RANK + 16, features // 4)],
        10,
        in_specs=[SMEM] * 2 + [VMEM] * len(others),
        out_specs=[VMEM] * 5,
        scratch_shapes=[pltpu.VMEM((2 * half, features), bf16), pltpu.VMEM((4, RANK, 2 * (features // 4)), bf16)],
    )(y, core, *others)


def input_gradient_kernel(delta_gate, delta_up, gate, up, mine, away):
    half = mine.shape[0]
    for part in parts(gate.shape[1]):
        total = dot(delta_gate[...], gate[:, part]) + dot(delta_up[...], up[:, part])
        total = total.astype(bf16)
        mine[:, part] = total[:half]
        away[:, part] = total[half:]


def input_gradient_of(delta_gate, delta_up, gate, up):
    rows = delta_gate.shape[0] // 2
    return call(
        input_gradient_kernel,
        "input_gradient",
        [shape(rows, gate.shape[1])] * 2,
        5,
        flops=8 * rows * gate.size,
        in_specs=[VMEM] * 4,
        out_specs=[VMEM, VMEM],
    )(delta_gate, delta_up, gate, up)


def core_sum_kernel(away, own, got, local, away_out, out0, out1, out2, out3):
    away_out[...] = away[...]
    for k, out in enumerate((out0, out1, out2, out3)):
        total = own[k].astype(f32) + got[k].astype(f32)
        folded = local[k, pl.ds(RANK, 16), :].astype(f32)
        out[pl.ds(0, SHARED), :] = jnp.concatenate([total[: SHARED - 8], folded[:8]], axis=0).astype(bf16)
        out[pl.ds(SHARED, RANK), :] = local[k, pl.ds(0, RANK), :]


def core_sum(away, own, got, local):
    return call(
        core_sum_kernel,
        "core_sum",
        [shape(*away.shape)] + [shape(SHARED + RANK, own.shape[2])] * 4,
        4,
        in_specs=[VMEM] * 4,
        out_specs=[VMEM] * 5,
    )(away, own, got, local)


def after_y_kernel(zl, after, own, a, b, c, out0, out1, out2, out3, shared):
    total = own[...].astype(f32) + a[...].astype(f32) + b[...].astype(f32) + c[...].astype(f32)
    wide = out0.shape[1]
    quarter = total.shape[1] // 4
    here = zl[0]
    for j in range(4):
        shared[j, :, pl.ds(0, quarter)] = total[:SHARED, j * quarter : (j + 1) * quarter]
    folded = total[SHARED - 8 : SHARED]
    rest = jnp.concatenate([folded[:, i * quarter : (i + 1) * quarter] for i in range(4)], axis=0)
    local = jnp.concatenate([total[SHARED:], rest], axis=1).astype(bf16)
    rest = local[:, 3 * wide :].astype(f32)
    rest = jnp.concatenate([rest, jnp.zeros((SHARED - RANK, rest.shape[1]), f32)], axis=0)
    shared[4, :, pl.ds(0, 128)] = jnp.zeros((SHARED, 128), f32)
    shared[4, :, pl.ds(128, 128)] = jnp.zeros((SHARED, 128), f32)
    shared[4, :, pl.ds(0, rest.shape[1])] = rest
    rest = pltpu.roll(shared[4], quarter, 1)
    lane = lax.broadcasted_iota(jnp.int32, rest.shape, 1)
    for k, out in enumerate((out0, out1, out2, out3)):
        out[pl.ds(0, SHARED), :] = jnp.where(lane < quarter, shared[here ^ k], rest).astype(bf16)
        for i in range(3):
            out[pl.ds(SHARED + i * RANK, RANK), :] = local[:, i * wide : (i + 1) * wide]


def after_y(zl, after, own, others):
    return call(
        after_y_kernel,
        "after_y",
        [shape(SHARED + 3 * RANK, 256)] * 4,
        4,
        flops=3000000000,
        in_specs=[SMEM, ANY] + [VMEM] * 4,
        out_specs=[VMEM] * 4,
        scratch_shapes=[pltpu.VMEM((5, SHARED, 256), f32)],
    )(zl, after, own, *others)


def after_z_kernel(after, own, a, b, c, shared, local):
    total = own[...].astype(f32) + a[...].astype(f32) + b[...].astype(f32) + c[...].astype(f32)
    shared[...] = total[:SHARED, : shared.shape[1]]
    wide = own.shape[1]
    for i in range(3):
        first = SHARED + i * RANK
        local[:, pl.ds(i * wide, wide)] = total[first : first + RANK].astype(bf16)
    quarter = shared.shape[1]
    width = local.shape[1] - 3 * wide
    local[:, pl.ds(3 * wide, width)] = total[:RANK, quarter : quarter + width].astype(bf16)


def after_z(after, own, others, quarter, units):
    return call(
        after_z_kernel,
        "after_z",
        [shape(SHARED, quarter, dtype=f32), shape(RANK, units)],
        4,
        flops=3000000000,
        in_specs=[ANY] + [VMEM] * 4,
        out_specs=[VMEM] * 2,
    )(after, own, *others)


def x_sum_kernel(after, own, a, b, c, out, sent):
    total = own[...] + a[...].astype(f32) + b[...].astype(f32) + c[...].astype(f32)
    out[...] = total
    sent[...] = total.astype(bf16)


def x_sum(after, own, others):
    return call(
        x_sum_kernel,
        "x_sum",
        [shape(*own.shape, dtype=f32), shape(*own.shape)],
        4,
        in_specs=[ANY] + [VMEM] * 4,
        out_specs=[VMEM] * 2,
    )(after, own, *others)


def half_sum_kernel(p_mine, p_got, i_mine, i_got, pair, one, two, three):
    part = p_mine.shape[0] // 4
    for place, mine, got in ((0, p_mine, p_got), (part, i_mine, i_got)):
        rows = pl.ds(place, part)
        total = mine[...].astype(f32) + got[...].astype(f32)
        pair[rows, :] = total[:part]
        for i, out in enumerate((one, two, three)):
            out[rows, :] = total[(i + 1) * part : (i + 2) * part].astype(bf16)


def half_sum(p_mine, p_got, i_mine, i_got):
    rows, features = p_mine.shape
    part = rows // 2
    return call(
        half_sum_kernel,
        "half_sum",
        [shape(part, features, dtype=f32)] + [shape(part, features)] * 3,
        5,
        in_specs=[VMEM] * 4,
        out_specs=[VMEM] * 4,
    )(p_mine, p_got, i_mine, i_got)


def pair_sum_kernel(pair, a, b, c, own, sent):
    total = pair[...] + a[...].astype(f32) + b[...].astype(f32) + c[...].astype(f32)
    rows = total.shape[0] // 4
    for i in range(2):
        first = 2 * i * rows
        own[pl.ds(i * rows, rows), :] = total[first : first + rows]
        sent[pl.ds(i * rows, rows), :] = total[first + rows : first + 2 * rows].astype(bf16)


def pair_sum(pair, got):
    rows, features = pair.shape
    return call(
        pair_sum_kernel,
        "pair_sum",
        [shape(rows // 2, features, dtype=f32), shape(rows // 2, features)],
        4,
        in_specs=[VMEM] * 4,
        out_specs=[VMEM] * 2,
    )(pair, *got)


def finish_kernel(
    y, place, core, row_own, row_got, d_sq, m_down, shared, shared_got, own, a, b, c,
    outputs, input_gradient, gate_in, up_in, gate, up, down, down_in, gate_m, up_m, down_m, held,
):
    rows = outputs.shape[0]
    total = row_own[...] + row_got[...].astype(f32)
    scale_down = m_down[...] / jnp.sqrt(d_sq[...] + epsilon)
    outputs[...] = (total[:rows] * scale_down).astype(bf16)
    input_gradient[...] = total[rows:].astype(bf16)
    for k, piece in enumerate((own, a, b, c)):
        held[k] = piece[...]
    here = y[0]
    for j, out in enumerate((gate, up, down)):
        out[...] = held[here ^ j].astype(f32)
    stats = held[here ^ 3][:16].astype(f32)
    gate_m[...] = stats[0]
    up_m[...] = stats[1]
    wide = gate_in.shape[0]
    first = core[0] == 0
    halves = jnp.where(first, shared[...], shared_got[...]), jnp.where(first, shared_got[...], shared[...])
    spots = (16, shared.shape[1])
    row = lax.broadcasted_iota(jnp.int32, spots, 0)
    chosen = (lax.broadcasted_iota(jnp.int32, spots, 1) == place[0] * wide + row).astype(f32)
    highest = lax.Precision.HIGHEST
    last = (((1,), (1,)), ((), ()))
    one, two = [lax.dot_general(chosen, h, last, precision=highest, preferred_element_type=f32) for h in halves]
    gate_in[...] = one[:wide, :RANK]
    up_in[...] = two[:wide, :RANK]
    down_in[:, pl.ds(0, 16)] = one[:wide, RANK : RANK + 16]
    down_in[:, pl.ds(16, 16)] = two[:wide, RANK : RANK + 16]
    line = lax.dot_general(halves[1][48:56], chosen, last, precision=highest, preferred_element_type=f32)
    down_m[...] = line[:1, :wide]


def finish(y, place, core, row_own, row_got, d_sq, m_down, shared, shared_got, own, others):
    rows, features = row_own.shape
    wide = shared.shape[1] // 16
    units = own.shape[1]
    small = shape(wide, RANK, dtype=f32)
    local = shape(RANK, units, dtype=f32)
    line = shape(units, dtype=f32)
    return call(
        finish_kernel,
        "finish",
        [shape(rows // 2, features)] * 2 + [small] * 2 + [local] * 3 + [small, line, line, shape(1, wide, dtype=f32)],
        6,
        in_specs=[SMEM] * 3 + [VMEM] * 10,
        out_specs=[VMEM] * 11,
        scratch_shapes=[pltpu.VMEM((4, RANK, units), bf16)],
    )(y, place, core, row_own, row_got, d_sq, m_down, shared, shared_got, own, *others)


def join_cot_kernel(after, pair, a, b, c, out):
    rows = pair.shape[0]
    for i, piece in enumerate((pair, a, b, c)):
        out[pl.ds(i * rows, rows), :] = piece[:rows]


def join_cot(after, pair, got):
    return call(
        join_cot_kernel,
        "join_cot",
        shape(4 * pair.shape[0], pair.shape[1]),
        4,
        in_specs=[ANY] + [VMEM] * 4,
        out_specs=VMEM,
    )(after, pair, *got)


def held_until_kernel(after, value, out):
    out[...] = value[...]


def held_until(after, value):
    return call(
        held_until_kernel,
        "held_until",
        shape(*value.shape, dtype=value.dtype),
        2,
        in_specs=[ANY, VMEM],
        out_specs=VMEM,
    )(after, value)


def split(value):
    high = value.astype(bf16)
    return jnp.concatenate([high, (value - high.astype(f32)).astype(bf16)], axis=0)


def joined(rows):
    return rows[0:1].astype(f32) + rows[1:2].astype(f32)


def shards(
    inputs, gate_weight, up_weight, down_weight, gate_adapter_in, b_gate, upper_adapter_in, b_up,
    down_adapter_in, b_down, m_gate, m_up, m_down, cotangent,
):
    rows, features = inputs.shape
    units = down_weight.shape[0]
    y, zl, core = lax.axis_index("y")[None], lax.axis_index("zl")[None], lax.axis_index("c")[None]
    place = (lax.axis_index("zh") * 4 + lax.axis_index("x")) * 2 + lax.axis_index("c")
    m_gate, m_up, m_down = m_gate[None], m_up[None], m_down[None]
    gate_t, up_t = gate_weight.T, up_weight.T
    ga_t, ua_t, ad_t = gate_adapter_in.T, upper_adapter_in.T, down_adapter_in.T

    other = swap_z(inputs)
    squares = down_squares(down_weight, ad_t, b_down)
    squares = held_until(other, squares)
    squares = squares + swap_core(squares)
    got = swap_z(jnp.concatenate([cotangent, split(squares)], axis=0))
    pair = jnp.concatenate([inputs, other], axis=0)
    got_x = swap_x(pair)
    mine = jnp.concatenate([pair] + got_x, axis=0)
    squares = squares + joined(got[rows:])
    pair = jnp.concatenate([cotangent, got[:rows]], axis=0)
    got = swap_x(jnp.concatenate([pair, split(squares)], axis=0))

    gate, up, down, g_scale, u_scale = merge(
        mine, gate_t, up_t, down_weight, ga_t, ua_t, b_gate, b_up, ad_t, b_down, m_gate, m_up
    )
    away = swap_core(mine)
    cot_mine = join_cot(g_scale, pair, got)
    cot_away = swap_core(cot_mine)
    squares = squares + sum(joined(g[2 * rows :]) for g in got)
    p_mine, p_away, hidden, gate_value, up_value, rank_in_t, rank_down_t = forward(
        cot_mine, mine, away, gate, up, down, ga_t, ua_t, ad_t, g_scale, u_scale
    )
    p_got = swap_core(p_away)

    delta_gate, delta_up, shared_own, shared_away, local = backward(
        y, core, cot_mine, cot_away, mine, away, p_mine, p_away, down, hidden, gate_value, up_value,
        rank_in_t, rank_down_t, b_down, b_gate, b_up, g_scale, u_scale, m_gate, m_up, squares, m_down,
    )
    i_mine, i_away = input_gradient_of(delta_gate, delta_up, gate, up)
    i_away, *packed = core_sum(i_away, shared_own, swap_core(shared_away), local)
    pair, *sent = half_sum(p_mine, p_got, i_mine, swap_core(i_away))
    own, *sent_z = after_y(zl, pair, packed[0], [swap(packed[k], "y", k, 4) for k in (1, 2, 3)])

    row_own, sent = pair_sum(pair, [swap(v, "x", k, 4) for k, v in zip(X_ORDER, sent)])
    row_got = swap_z(sent)

    quarter = features // 16
    shared, local = after_z(packed[0], own, [swap(v, "zl", k + 1, 4) for k, v in enumerate(sent_z)], quarter, units)
    others = [swap(local, "y", k, 4) for k in (1, 2, 3)]
    shared, sent_zh = x_sum(row_got, shared, swap_x(shared.astype(bf16)))
    shared = shared + swap(sent_zh, "zh", 1, 2).astype(f32)
    outputs, input_gradient, gate_in, up_in, gate_out, up_out, down_out, down_in, gate_m, up_m, down_m = finish(
        y, place[None], core, row_own, row_got, squares, m_down, shared, swap_core(shared), local, others
    )
    return (
        outputs,
        input_gradient,
        gate_in,
        up_in,
        gate_out,
        up_out,
        down_out.T,
        down_in.T,
        gate_m,
        up_m,
        down_m[0],
    )


def solution(mesh):
    fine = Mesh(mesh.devices.reshape(4, 4, 2, 4, 2), ALL)
    return jax.shard_map(
        shards,
        mesh=fine,
        in_specs=(
            P(ALL, None),
            P(None, TENSOR),
            P(None, TENSOR),
            P(TENSOR, None),
            P(),
            P(None, TENSOR),
            P(),
            P(None, TENSOR),
            P(TENSOR, None),
            P(),
            P(TENSOR),
            P(TENSOR),
            P(),
            P(ALL, None),
        ),
        out_specs=(
            P(ALL, None),
            P(ALL, None),
            P(ALL, None),
            P(ALL, None),
            P(None, TENSOR),
            P(None, TENSOR),
            P(TENSOR, None),
            P(None, ALL),
            P(TENSOR),
            P(TENSOR),
            P(ALL),
        ),
        check_vma=False,
    )
```

```python
import jax
import jax.numpy as jnp
from jax import lax
from jax.experimental import pallas as pl
from jax.experimental.pallas import tpu as pltpu
from jax.sharding import Mesh, PartitionSpec as P

adapter_scale = 2.0
epsilon = 1e-06
bf16 = jnp.bfloat16
f32 = jnp.float32

DATA = ("y", "zl")
TENSOR = ("zh", "x", "c")
ALL = DATA + TENSOR
X_ORDER = (1, 3, 2)
FAR_FIRST = (2, 1, 3)
MIB = 1024 * 1024
ANY = pl.BlockSpec(memory_space=pl.ANY)
VMEM = pl.BlockSpec(memory_space=pltpu.VMEM)
SMEM = pl.BlockSpec(memory_space=pltpu.SMEM)
SPANS = ((0, 256), (256, 256), (512, 288))
WIDE = 640
RANK = 32
SHARED = 64


def swap(value, axis, distance, size):
    return lax.ppermute(value, axis, [(i, i ^ distance) for i in range(size)])


def swap_core(value):
    return swap(value, "c", 1, 2)


def swap_z(value):
    return swap(value, ("zl", "zh"), 5, 8)


def swap_x(value):
    return [swap(value, "x", k, 4) for k in X_ORDER]


def dot(a, b):
    return jnp.dot(a, b, preferred_element_type=f32)


def dot_last(a, b):
    return lax.dot_general(a, b, (((1,), (1,)), ((), ())), preferred_element_type=f32)


def dot_first(a, b):
    return lax.dot_general(a, b, (((0,), (0,)), ((), ())), preferred_element_type=f32)


def shape(*dims, dtype=bf16):
    return jax.ShapeDtypeStruct(dims, dtype)


def call(kernel, name, out_shape, mib, flops=1000, **kwargs):
    return pl.pallas_call(
        kernel,
        out_shape=out_shape,
        compiler_params=pltpu.CompilerParams(vmem_limit_bytes=mib * MIB),
        cost_estimate=pl.CostEstimate(flops=flops, bytes_accessed=1000, transcendentals=0),
        name=name,
        **kwargs,
    )


def parts(features):
    return [pl.ds(i, WIDE) for i in range(0, features, WIDE)]


class Copies:
    def __init__(self, pairs, sems, ahead):
        self.copies = [pltpu.make_async_copy(a, b, sems.at[i]) for i, (a, b) in enumerate(pairs)]
        self.started = self.waited = 0
        self.ahead = ahead
        self.fill()

    def fill(self):
        while self.started < min(len(self.copies), self.waited + self.ahead):
            self.copies[self.started].start()
            self.started += 1

    def wait(self):
        self.copies[self.waited].wait()
        self.waited += 1
        self.fill()


def down_squares_kernel(w_ref, a_ref, b_ref, squares_ref, w, a, b, sems):
    spans = parts(w_ref.shape[1])
    pairs = [(a_ref, a), (b_ref, b)] + [(w_ref.at[:, part], w.at[:, part]) for part in spans]
    copies = Copies(pairs, sems, len(pairs))
    copies.wait()
    copies.wait()
    for part in spans:
        copies.wait()
        merged = w[:, part].astype(f32) + adapter_scale * dot_first(a[...], b[:, part])
        squares_ref[:, part] = jnp.sum(merged * merged, axis=0, keepdims=True)


def down_squares(weight, left_t, right):
    return call(
        down_squares_kernel,
        "down_squares",
        shape(1, weight.shape[1], dtype=f32),
        56,
        in_specs=[ANY] * 3,
        out_specs=VMEM,
        scratch_shapes=[
            pltpu.VMEM(weight.shape, bf16),
            pltpu.VMEM(left_t.shape, bf16),
            pltpu.VMEM(right.shape, bf16),
            pltpu.SemaphoreType.DMA((2 + weight.shape[1] // WIDE,)),
        ],
    )(weight, left_t, right)


def merge_kernel(
    after, g_ref, u_ref, d_ref, ga, ua, gb, ub, ad, bd, g_m, u_m, g_out, u_out, d_out, g_scale, u_scale,
    g_held, u_held, d_held, sems,
):
    spans = parts(g_ref.shape[1])
    pairs = []
    for part in (pl.ds(0, 2 * WIDE), pl.ds(2 * WIDE, 2 * WIDE)):
        pairs.append((g_ref.at[:, part], g_held.at[:, part]))
    pairs += [(u_ref, u_held), (d_ref, d_held)]
    copies = Copies(pairs, sems, len(pairs))
    for w, a, b, m, out, scale in ((g_held, ga, gb, g_m, g_out, g_scale), (u_held, ua, ub, u_m, u_out, u_scale)):
        squares = 0.0
        for n, part in enumerate(spans):
            if n == 0 or (n == 2 and w is g_held):
                copies.wait()
            merged = w[:, part].astype(f32) + adapter_scale * dot_first(b[...], a[:, part])
            out[:, part] = merged.astype(bf16)
            square = merged * merged
            squares += sum(square[:, k : k + 128] for k in range(0, WIDE, 128))
        total = jnp.sum(jnp.transpose(squares), axis=0, keepdims=True)
        scale[...] = m[...] / jnp.sqrt(total + epsilon)
    copies.wait()
    for part in spans:
        merged = d_held[:, part].astype(f32) + adapter_scale * dot_first(ad[...], bd[:, part])
        d_out[:, part] = merged.astype(bf16)


def merge(after, gate, up, down, *others):
    units, features = gate.shape
    return call(
        merge_kernel,
        "merge",
        [shape(*gate.shape)] * 3 + [shape(1, units, dtype=f32)] * 2,
        40,
        in_specs=[ANY] * 4 + [VMEM] * len(others),
        out_specs=[VMEM] * 5,
        scratch_shapes=[pltpu.VMEM(gate.shape, bf16)] * 3 + [pltpu.SemaphoreType.DMA((4,))],
    )(after, gate, up, down, *others)


def forward_kernel(
    after, mine, away, gate, up, down, ga_t, ua_t, ad_t, g_scale, u_scale,
    p_mine, p_away, hidden_out, gate_out, up_out, rank_in_t, rank_down_t, rows,
):
    half = mine.shape[0]
    rows[:half] = mine[...]
    rows[half:] = away[...]
    rank_down = 0.0
    for start, size in SPANS:
        span = pl.ds(start, size)
        gate_value = dot_last(rows[...], gate[span, :]) * g_scale[:, span]
        up_value = dot_last(rows[...], up[span, :]) * u_scale[:, span]
        gate_out[:, span] = gate_value.astype(bf16)
        up_out[:, span] = up_value.astype(bf16)
        hidden = (gate_value * jax.nn.sigmoid(gate_value) * up_value).astype(bf16)
        hidden_out[:, span] = hidden
        rank_down += dot_last(ad_t[:, span], hidden)
    rank_down_t[...] = rank_down.astype(bf16)
    for part in parts(down.shape[1]):
        p = dot(hidden_out[...], down[:, part]).astype(bf16)
        p_mine[:, part] = p[:half]
        p_away[:, part] = p[half:]
    rank_in_t[:RANK, :] = dot_last(ga_t[...], rows[...]).astype(bf16)
    rank_in_t[RANK:, :] = dot_last(ua_t[...], rows[...]).astype(bf16)


def forward(after, mine, *others):
    half, features = mine.shape
    units = others[1].shape[0]
    return call(
        forward_kernel,
        "forward",
        [shape(half, features)] * 2 + [shape(2 * half, units)] * 3 + [shape(2 * RANK, 2 * half), shape(RANK, 2 * half)],
        6,
        in_specs=[ANY] + [VMEM] * (1 + len(others)),
        out_specs=[VMEM] * 7,
        scratch_shapes=[pltpu.VMEM((2 * half, features), bf16)],
    )(after, mine, *others)


def backward_kernel(
    y, core, cot_mine, cot_away, mine, away, p_mine, p_away, down, hidden, gate_value, up_value,
    rank_in_t, rank_down_t, b_down, b_gate, b_up, g_scale, u_scale, m_gate, m_up, d_sq, m_down,
    delta_gate_out, delta_up_out, shared_own, shared_away, local_out,
    delta, local,
):
    units, features = down.shape
    half = mine.shape[0]
    block = features // 4
    norm_down = jnp.sqrt(d_sq[...] + epsilon)
    scale_down = m_down[...] / norm_down
    delta[:half] = (cot_mine[...].astype(f32) * scale_down).astype(bf16)
    delta[half:] = (cot_away[...].astype(f32) * scale_down).astype(bf16)
    back_down_t = dot_last(b_down[...], delta[...]).astype(bf16)
    back_gate = back_up = 0.0
    local[:, :, pl.ds(768, 512)] = jnp.zeros((4, RANK, 512), bf16)
    for start, size in SPANS:
        span = pl.ds(start, size)
        grad_hidden = dot_last(delta[...], down[span, :])
        gate = gate_value[:, span].astype(f32)
        upper = up_value[:, span].astype(f32)
        logistic = jax.nn.sigmoid(gate)
        activated = gate * logistic
        grad_up = grad_hidden * activated
        grad_gate = grad_hidden * upper * (logistic + activated * (1.0 - logistic))
        grad_m_gate = jnp.sum(grad_gate * gate, axis=0, keepdims=True) / m_gate[:, span]
        grad_m_up = jnp.sum(grad_up * upper, axis=0, keepdims=True) / m_up[:, span]
        delta_gate = (grad_gate * g_scale[:, span]).astype(bf16)
        delta_up = (grad_up * u_scale[:, span]).astype(bf16)
        delta_gate_out[:, span] = delta_gate
        delta_up_out[:, span] = delta_up
        back_gate += dot_last(b_gate[:, span], delta_gate)
        back_up += dot_last(b_up[:, span], delta_up)
        local[0, :, span] = (adapter_scale * dot(rank_in_t[:RANK, :], delta_gate)).astype(bf16)
        local[1, :, span] = (adapter_scale * dot(rank_in_t[RANK:, :], delta_up)).astype(bf16)
        local[2, :, span] = (adapter_scale * dot(back_down_t, hidden[:, span])).astype(bf16)
        stats = jnp.concatenate([grad_m_gate, grad_m_up, jnp.zeros((RANK - 2, size), f32)], axis=0)
        local[3, :, span] = stats.astype(bf16)
    back_t = jnp.concatenate([back_gate, back_up], axis=0).astype(bf16)
    here = y[0]
    first = core[0] == 0
    for k in range(4):
        chunk = here ^ k
        part = pl.ds(pl.multiple_of(chunk * block, 128), block)
        own = local[chunk]
        folded = sum(
            pltpu.roll(own[i * 8 : (i + 1) * 8, block:].astype(f32), i * (units - block), 1) for i in range(4)
        )
        local_out[k, pl.ds(0, RANK), :] = own[:, :block]
        folded = jnp.concatenate([folded, jnp.zeros((8, block), f32)], axis=0)
        local_out[k, pl.ds(RANK, 16), :] = folded.astype(bf16)
        back_rows = adapter_scale * (dot(back_t[:, :half], mine[:, part]) + dot(back_t[:, half:], away[:, part]))
        down_rows = adapter_scale * dot(rank_down_t[...], delta[:, part])
        moment = sum(
            jnp.sum(cot[:, part].astype(f32) * partial[:, part].astype(f32), axis=0, keepdims=True)
            for cot, partial in ((cot_mine, p_mine), (cot_away, p_away))
        )
        moment = moment / jnp.sqrt(d_sq[:, part] + epsilon)
        zeros = jnp.zeros((15, block), f32)
        one = jnp.concatenate([back_rows[:RANK], down_rows[:16], jnp.zeros((16, block), f32)], axis=0)
        two = jnp.concatenate([back_rows[RANK:], down_rows[16:], moment, zeros], axis=0)
        shared_own[k] = jnp.where(first, one, two).astype(bf16)
        shared_away[k] = jnp.where(first, two, one).astype(bf16)


def backward(y, core, *others):
    half, features = others[0].shape
    units = others[6].shape[0]
    return call(
        backward_kernel,
        "backward",
        [shape(2 * half, units)] * 2 + [shape(4, SHARED, features // 4)] * 2 + [shape(4, RANK + 16, features // 4)],
        10,
        in_specs=[SMEM] * 2 + [VMEM] * len(others),
        out_specs=[VMEM] * 5,
        scratch_shapes=[pltpu.VMEM((2 * half, features), bf16), pltpu.VMEM((4, RANK, 2 * (features // 4)), bf16)],
    )(y, core, *others)


def input_gradient_kernel(delta_gate, delta_up, gate, up, mine, away):
    half = mine.shape[0]
    for part in parts(gate.shape[1]):
        total = dot(delta_gate[...], gate[:, part]) + dot(delta_up[...], up[:, part])
        total = total.astype(bf16)
        mine[:, part] = total[:half]
        away[:, part] = total[half:]


def input_gradient_of(delta_gate, delta_up, gate, up):
    rows = delta_gate.shape[0] // 2
    return call(
        input_gradient_kernel,
        "input_gradient",
        [shape(rows, gate.shape[1])] * 2,
        5,
        flops=8 * rows * gate.size,
        in_specs=[VMEM] * 4,
        out_specs=[VMEM, VMEM],
    )(delta_gate, delta_up, gate, up)


def core_sum_kernel(away, own, got, local, away_out, out0, out1, out2, out3):
    away_out[...] = away[...]
    for k, out in enumerate((out0, out1, out2, out3)):
        total = own[k].astype(f32) + got[k].astype(f32)
        folded = local[k, pl.ds(RANK, 16), :].astype(f32)
        out[pl.ds(0, SHARED), :] = jnp.concatenate([total[: SHARED - 8], folded[:8]], axis=0).astype(bf16)
        out[pl.ds(SHARED, RANK), :] = local[k, pl.ds(0, RANK), :]


def core_sum(away, own, got, local):
    return call(
        core_sum_kernel,
        "core_sum",
        [shape(*away.shape)] + [shape(SHARED + RANK, own.shape[2])] * 4,
        4,
        in_specs=[VMEM] * 4,
        out_specs=[VMEM] * 5,
    )(away, own, got, local)


def after_y_kernel(zl, after, own, a, b, c, out0, out1, out2, out3, shared):
    total = own[...].astype(f32) + a[...].astype(f32) + b[...].astype(f32) + c[...].astype(f32)
    wide = out0.shape[1]
    quarter = total.shape[1] // 4
    here = zl[0]
    for j in range(4):
        shared[j, :, pl.ds(0, quarter)] = total[:SHARED, j * quarter : (j + 1) * quarter]
    folded = total[SHARED - 8 : SHARED]
    rest = jnp.concatenate([folded[:, i * quarter : (i + 1) * quarter] for i in range(4)], axis=0)
    local = jnp.concatenate([total[SHARED:], rest], axis=1).astype(bf16)
    rest = local[:, 3 * wide :].astype(f32)
    rest = jnp.concatenate([rest, jnp.zeros((SHARED - RANK, rest.shape[1]), f32)], axis=0)
    shared[4, :, pl.ds(0, 128)] = jnp.zeros((SHARED, 128), f32)
    shared[4, :, pl.ds(128, 128)] = jnp.zeros((SHARED, 128), f32)
    shared[4, :, pl.ds(0, rest.shape[1])] = rest
    rest = pltpu.roll(shared[4], quarter, 1)
    lane = lax.broadcasted_iota(jnp.int32, rest.shape, 1)
    for k, out in enumerate((out0, out1, out2, out3)):
        out[pl.ds(0, SHARED), :] = jnp.where(lane < quarter, shared[here ^ k], rest).astype(bf16)
        for i in range(3):
            out[pl.ds(SHARED + i * RANK, RANK), :] = local[:, i * wide : (i + 1) * wide]


def after_y(zl, after, own, others):
    return call(
        after_y_kernel,
        "after_y",
        [shape(SHARED + 3 * RANK, 256)] * 4,
        4,
        flops=3000000000,
        in_specs=[SMEM, ANY] + [VMEM] * 4,
        out_specs=[VMEM] * 4,
        scratch_shapes=[pltpu.VMEM((5, SHARED, 256), f32)],
    )(zl, after, own, *others)


def after_z_kernel(after, own, a, b, c, shared, local):
    total = own[...].astype(f32) + a[...].astype(f32) + b[...].astype(f32) + c[...].astype(f32)
    shared[...] = total[:SHARED, : shared.shape[1]]
    wide = own.shape[1]
    for i in range(3):
        first = SHARED + i * RANK
        local[:, pl.ds(i * wide, wide)] = total[first : first + RANK].astype(bf16)
    quarter = shared.shape[1]
    width = local.shape[1] - 3 * wide
    local[:, pl.ds(3 * wide, width)] = total[:RANK, quarter : quarter + width].astype(bf16)


def after_z(after, own, others, quarter, units):
    return call(
        after_z_kernel,
        "after_z",
        [shape(SHARED, quarter, dtype=f32), shape(RANK, units)],
        4,
        flops=3000000000,
        in_specs=[ANY] + [VMEM] * 4,
        out_specs=[VMEM] * 2,
    )(after, own, *others)


def x_sum_kernel(after, own, a, b, c, out, sent):
    total = own[...] + a[...].astype(f32) + b[...].astype(f32) + c[...].astype(f32)
    out[...] = total
    sent[...] = total.astype(bf16)


def x_sum(after, own, others):
    return call(
        x_sum_kernel,
        "x_sum",
        [shape(*own.shape, dtype=f32), shape(*own.shape)],
        4,
        in_specs=[ANY] + [VMEM] * 4,
        out_specs=[VMEM] * 2,
    )(after, own, *others)


def half_sum_kernel(p_mine, p_got, i_mine, i_got, pair, one, two, three):
    part = p_mine.shape[0] // 4
    for place, mine, got in ((0, p_mine, p_got), (part, i_mine, i_got)):
        rows = pl.ds(place, part)
        total = mine[...].astype(f32) + got[...].astype(f32)
        pair[rows, :] = total[:part]
        for i, out in enumerate((one, two, three)):
            out[rows, :] = total[(i + 1) * part : (i + 2) * part].astype(bf16)


def half_sum(p_mine, p_got, i_mine, i_got):
    rows, features = p_mine.shape
    part = rows // 2
    return call(
        half_sum_kernel,
        "half_sum",
        [shape(part, features, dtype=f32)] + [shape(part, features)] * 3,
        5,
        in_specs=[VMEM] * 4,
        out_specs=[VMEM] * 4,
    )(p_mine, p_got, i_mine, i_got)


def pair_sum_kernel(pair, a, b, c, own, sent):
    total = pair[...] + a[...].astype(f32) + b[...].astype(f32) + c[...].astype(f32)
    rows = total.shape[0] // 4
    for i in range(2):
        first = 2 * i * rows
        own[pl.ds(i * rows, rows), :] = total[first : first + rows]
        sent[pl.ds(i * rows, rows), :] = total[first + rows : first + 2 * rows].astype(bf16)


def pair_sum(pair, got):
    rows, features = pair.shape
    return call(
        pair_sum_kernel,
        "pair_sum",
        [shape(rows // 2, features, dtype=f32), shape(rows // 2, features)],
        4,
        in_specs=[VMEM] * 4,
        out_specs=[VMEM] * 2,
    )(pair, *got)


def finish_kernel(
    y, place, core, row_own, row_got, d_sq, m_down, shared, shared_got, own, a, b, c,
    outputs, input_gradient, gate_in, up_in, gate, up, down, down_in, gate_m, up_m, down_m, held,
):
    rows = outputs.shape[0]
    total = row_own[...] + row_got[...].astype(f32)
    scale_down = m_down[...] / jnp.sqrt(d_sq[...] + epsilon)
    outputs[...] = (total[:rows] * scale_down).astype(bf16)
    input_gradient[...] = total[rows:].astype(bf16)
    for k, piece in enumerate((own, a, b, c)):
        held[k] = piece[...]
    here = y[0]
    for j, out in enumerate((gate, up, down)):
        out[...] = held[here ^ j].astype(f32)
    stats = held[here ^ 3][:16].astype(f32)
    gate_m[...] = stats[0]
    up_m[...] = stats[1]
    wide = gate_in.shape[0]
    first = core[0] == 0
    halves = jnp.where(first, shared[...], shared_got[...]), jnp.where(first, shared_got[...], shared[...])
    spots = (16, shared.shape[1])
    row = lax.broadcasted_iota(jnp.int32, spots, 0)
    chosen = (lax.broadcasted_iota(jnp.int32, spots, 1) == place[0] * wide + row).astype(f32)
    highest = lax.Precision.HIGHEST
    last = (((1,), (1,)), ((), ()))
    one, two = [lax.dot_general(chosen, h, last, precision=highest, preferred_element_type=f32) for h in halves]
    gate_in[...] = one[:wide, :RANK]
    up_in[...] = two[:wide, :RANK]
    down_in[:, pl.ds(0, 16)] = one[:wide, RANK : RANK + 16]
    down_in[:, pl.ds(16, 16)] = two[:wide, RANK : RANK + 16]
    line = lax.dot_general(halves[1][48:56], chosen, last, precision=highest, preferred_element_type=f32)
    down_m[...] = line[:1, :wide]


def finish(y, place, core, row_own, row_got, d_sq, m_down, shared, shared_got, own, others):
    rows, features = row_own.shape
    wide = shared.shape[1] // 16
    units = own.shape[1]
    small = shape(wide, RANK, dtype=f32)
    local = shape(RANK, units, dtype=f32)
    line = shape(units, dtype=f32)
    return call(
        finish_kernel,
        "finish",
        [shape(rows // 2, features)] * 2 + [small] * 2 + [local] * 3 + [small, line, line, shape(1, wide, dtype=f32)],
        6,
        in_specs=[SMEM] * 3 + [VMEM] * 10,
        out_specs=[VMEM] * 11,
        scratch_shapes=[pltpu.VMEM((4, RANK, units), bf16)],
    )(y, place, core, row_own, row_got, d_sq, m_down, shared, shared_got, own, *others)


def join_cot_kernel(after, pair, a, b, c, out):
    rows = pair.shape[0]
    for i, piece in enumerate((pair, a, b, c)):
        out[pl.ds(i * rows, rows), :] = piece[:rows]


def join_cot(after, pair, got):
    return call(
        join_cot_kernel,
        "join_cot",
        shape(4 * pair.shape[0], pair.shape[1]),
        4,
        in_specs=[ANY] + [VMEM] * 4,
        out_specs=VMEM,
    )(after, pair, *got)


def held_until_kernel(after, value, out):
    out[...] = value[...]


def held_until(after, value):
    return call(
        held_until_kernel,
        "held_until",
        shape(*value.shape, dtype=value.dtype),
        2,
        in_specs=[ANY, VMEM],
        out_specs=VMEM,
    )(after, value)


def split(value):
    high = value.astype(bf16)
    return jnp.concatenate([high, (value - high.astype(f32)).astype(bf16)], axis=0)


def joined(rows):
    return rows[0:1].astype(f32) + rows[1:2].astype(f32)


def shards(
    inputs, gate_weight, up_weight, down_weight, gate_adapter_in, b_gate, upper_adapter_in, b_up,
    down_adapter_in, b_down, m_gate, m_up, m_down, cotangent,
):
    rows, features = inputs.shape
    units = down_weight.shape[0]
    y, zl, core = lax.axis_index("y")[None], lax.axis_index("zl")[None], lax.axis_index("c")[None]
    place = (lax.axis_index("zh") * 4 + lax.axis_index("x")) * 2 + lax.axis_index("c")
    m_gate, m_up, m_down = m_gate[None], m_up[None], m_down[None]
    gate_t, up_t = gate_weight.T, up_weight.T
    ga_t, ua_t, ad_t = gate_adapter_in.T, upper_adapter_in.T, down_adapter_in.T

    other = swap_z(inputs)
    squares = down_squares(down_weight, ad_t, b_down)
    squares = held_until(other, squares)
    squares = squares + swap_core(squares)
    got = swap_z(jnp.concatenate([cotangent, split(squares)], axis=0))
    pair = jnp.concatenate([inputs, other], axis=0)
    got_x = swap_x(pair)
    mine = jnp.concatenate([pair] + got_x, axis=0)
    squares = squares + joined(got[rows:])
    pair = jnp.concatenate([cotangent, got[:rows]], axis=0)
    got = swap_x(jnp.concatenate([pair, split(squares)], axis=0))

    gate, up, down, g_scale, u_scale = merge(
        mine, gate_t, up_t, down_weight, ga_t, ua_t, b_gate, b_up, ad_t, b_down, m_gate, m_up
    )
    away = swap_core(mine)
    cot_mine = join_cot(g_scale, pair, got)
    cot_away = swap_core(cot_mine)
    squares = squares + sum(joined(g[2 * rows :]) for g in got)
    p_mine, p_away, hidden, gate_value, up_value, rank_in_t, rank_down_t = forward(
        cot_mine, mine, away, gate, up, down, ga_t, ua_t, ad_t, g_scale, u_scale
    )
    p_got = swap_core(p_away)

    delta_gate, delta_up, shared_own, shared_away, local = backward(
        y, core, cot_mine, cot_away, mine, away, p_mine, p_away, down, hidden, gate_value, up_value,
        rank_in_t, rank_down_t, b_down, b_gate, b_up, g_scale, u_scale, m_gate, m_up, squares, m_down,
    )
    i_mine, i_away = input_gradient_of(delta_gate, delta_up, gate, up)
    i_away, *packed = core_sum(i_away, shared_own, swap_core(shared_away), local)
    pair, *sent = half_sum(p_mine, p_got, i_mine, swap_core(i_away))
    own, *sent_z = after_y(zl, pair, packed[0], [swap(packed[k], "y", k, 4) for k in FAR_FIRST])

    row_own, sent = pair_sum(pair, [swap(v, "x", k, 4) for k, v in zip(X_ORDER, sent)])
    row_got = swap_z(sent)

    quarter = features // 16
    shared, local = after_z(packed[0], own, [swap(sent_z[k - 1], "zl", k, 4) for k in (1, 2, 3)], quarter, units)
    shared_sent = shared.astype(bf16)
    by_distance = {k: swap(local, "y", k, 4) for k in FAR_FIRST}
    others = [by_distance[k] for k in (1, 2, 3)]
    shared, sent_zh = x_sum(row_got, shared, [swap(shared_sent, "x", k, 4) for k in FAR_FIRST])
    shared = shared + swap(sent_zh, "zh", 1, 2).astype(f32)
    outputs, input_gradient, gate_in, up_in, gate_out, up_out, down_out, down_in, gate_m, up_m, down_m = finish(
        y, place[None], core, row_own, row_got, squares, m_down, shared, swap_core(shared), local, others
    )
    return (
        outputs,
        input_gradient,
        gate_in,
        up_in,
        gate_out,
        up_out,
        down_out.T,
        down_in.T,
        gate_m,
        up_m,
        down_m[0],
    )


def solution(mesh):
    fine = Mesh(mesh.devices.reshape(4, 4, 2, 4, 2), ALL)
    return jax.shard_map(
        shards,
        mesh=fine,
        in_specs=(
            P(ALL, None),
            P(None, TENSOR),
            P(None, TENSOR),
            P(TENSOR, None),
            P(),
            P(None, TENSOR),
            P(),
            P(None, TENSOR),
            P(TENSOR, None),
            P(),
            P(TENSOR),
            P(TENSOR),
            P(),
            P(ALL, None),
        ),
        out_specs=(
            P(ALL, None),
            P(ALL, None),
            P(ALL, None),
            P(ALL, None),
            P(None, TENSOR),
            P(None, TENSOR),
            P(TENSOR, None),
            P(None, ALL),
            P(TENSOR),
            P(TENSOR),
            P(ALL),
        ),
        check_vma=False,
    )
```
